256 devices in a mesh: ctx: 64 (over x, z, y_hi), tp: 4 (over y_lo, core).
Axes of the slice: x: 4, y: 4 (y_hi: 2, y_lo: 2; y = y_hi * 2 + y_lo), z: 8, core: 2. Of those that a mesh axis runs over, the one named last changes fastest.
Arguments:
- queries: bfloat16 [65536, 2048], P('ctx', 'tp'), may hold values from -6 to 6
- keys: bfloat16 [65536, 2048], P('ctx', 'tp'), may hold values from -6 to 6
- values: bfloat16 [65536, 2048], P('ctx', 'tp'), may hold values from -6 to 6
- offsets: int32 [32, 2], replicated, may hold values from 0 to 15
- out_weight: bfloat16 [2048, 2048], P('tp'), may hold values from -0.125 to 0.125
Outputs:
- mixed: bfloat16 [65536, 2048], P(('ctx', 'tp'))
The draws below stay inside these ranges and needn't reach their ends.
All inputs are finite; a program needn't handle non-finite values.
Results may differ from the reference program's by a relative error of at most 0.015.
Values may be sent and summed in bfloat16 or wider, within the bound.
No kernel may reach another device: no remote copies, remote signals or barrier semaphores. Data moves between devices by JAX's collectives and lax.ppermute only.
A program may use at most 128 MiB of HBM per device.

```python
import jax
import jax.numpy as jnp
from jax import lax

HEAD_COUNT = 32
HEAD_DIM = 64
D = 2048
TOKENS_PER_SHARD = 1024
SECOND_DILATION = 8
SECOND_SPAN = 8
THIRD_DILATION = 16
TOKEN_COUNT = 65536


def draw_queries(key, part):
    drawn_attention = jnp.clip(2.5 * jax.random.normal(jax.random.fold_in(key, 21), (TOKEN_COUNT, D), jnp.float32), -6.0, 6.0)
    return drawn_attention.astype(jnp.bfloat16)


def draw_keys(key, part):
    drawn_attention = jnp.clip(jax.random.normal(jax.random.fold_in(key, 22), (TOKEN_COUNT, D), jnp.float32), -4.0, 4.0)
    return drawn_attention.astype(jnp.bfloat16)


def touch_ends(entries, key, smallest, high):
    place = [jax.random.randint(jax.random.fold_in(key, axis), (), 0, length) for axis, length in enumerate(entries.shape)]
    widest = entries.shape.index(max(entries.shape))
    beside = place[:widest] + [(place[widest] + 1) % entries.shape[widest]] + place[widest + 1:]
    return entries.at[tuple(place)].set(smallest).at[tuple(beside)].set(high)


def levels(key, dims, pieces, least, top_value):
    loudness = 1.0
    for axis_at, blocks in pieces:
        steps = jax.random.uniform(jax.random.fold_in(jax.random.fold_in(key, 6), axis_at), (blocks,), jnp.float32, least / len(pieces), top_value / len(pieces))
        loudness = loudness * jnp.repeat(jnp.exp(steps), dims[axis_at] // blocks).reshape((-1,) + (1,) * (len(dims) - 1 - axis_at))
    return loudness


def scatter_about(rng, shape, width, limit, shards=(), dtype=jnp.bfloat16):
    values = jax.random.normal(rng, shape, jnp.float32) * width
    if len(shards) > 0:
        values = levels(rng, shape, shards, -0.22, 0.18) * values
    return jnp.clip(values, min=-limit, max=limit).astype(dtype)


def setup_inputs(seed: int = 0) -> dict:
    arg_keys = jax.random.split(jax.random.key(seed), 6)
    queries = draw_queries(jax.random.fold_in(arg_keys[5], 71), 0)
    keys = draw_keys(jax.random.fold_in(arg_keys[5], 71), 0)
    values = scatter_about(arg_keys[2], (TOKEN_COUNT, D), 1.0, 6.0, ((0, 64), (1, 4)))
    offsets = touch_ends(jax.random.randint(arg_keys[3], (HEAD_COUNT, 2), 0, THIRD_DILATION), jax.random.fold_in(arg_keys[3], 1), 0, THIRD_DILATION - 1).astype(jnp.int32)
    out_weight = scatter_about(arg_keys[4], (D, D), D ** -0.5, 0.125, ((0, 4),))
    return dict(queries=queries, keys=keys, values=values, offsets=offsets, out_weight=out_weight)


NEG = -1e30


def dilation_pattern(query_per_head, key_per_head, value_per_head, seg_len, dilation, start_offset):
    count = query_per_head.shape[0] // dilation

    def pick(field):
        chosen = lax.dynamic_index_in_dim(field.reshape(count, dilation, HEAD_DIM), start_offset, axis=1, keepdims=False)
        return chosen.reshape(query_per_head.shape[0] // seg_len, seg_len // dilation, HEAD_DIM)

    def segment(inputs):
        seg_q, seg_k, seg_v = inputs
        scores = jnp.dot(seg_q, seg_k.T, preferred_element_type=jnp.float32) * (HEAD_DIM ** -0.5)
        peak = jnp.max(scores, axis=1)
        expo = jnp.exp(scores - peak[:, None])
        total = jnp.sum(expo, axis=1)
        summed = jnp.dot(expo.astype(jnp.bfloat16), seg_v, preferred_element_type=jnp.float32)
        return peak, total, summed

    peak, total, summed = lax.map(segment, (pick(query_per_head), pick(key_per_head), pick(value_per_head)))
    peak = peak.reshape(count)
    total = total.reshape(count)
    summed = summed.reshape(count, HEAD_DIM)
    hit = jnp.arange(dilation)[None, :] == start_offset
    peak_full = jnp.where(hit, peak[:, None], NEG).reshape(-1)
    total_full = jnp.where(hit, total[:, None], 0.0).reshape(-1)
    summed_full = jnp.where(hit[:, :, None], summed[:, None, :], 0.0).reshape(-1, HEAD_DIM)
    return peak_full, total_full, summed_full


def reference(queries, keys, values, offsets, out_weight):
    def one_head(inputs):
        query_per_head, key_per_head, value_per_head, start_offset = inputs
        parts = [dilation_pattern(query_per_head, key_per_head, value_per_head, TOKENS_PER_SHARD, 1, 0),
                 dilation_pattern(query_per_head, key_per_head, value_per_head, TOKENS_PER_SHARD * SECOND_SPAN, SECOND_DILATION, start_offset[0] % SECOND_DILATION),
                 dilation_pattern(query_per_head, key_per_head, value_per_head, TOKEN_COUNT, THIRD_DILATION, start_offset[1] % THIRD_DILATION)]
        top = jnp.maximum(jnp.maximum(parts[0][0], parts[1][0]), parts[2][0])
        numer = jnp.zeros((query_per_head.shape[0], HEAD_DIM), jnp.float32)
        denom = jnp.zeros((query_per_head.shape[0],), jnp.float32)
        for peak, total, summed in parts:
            scale = jnp.exp(peak - top)
            numer = numer + scale[:, None] * summed
            denom = denom + scale * total
        return (numer / denom[:, None]).astype(jnp.bfloat16)

    def heads_first(field):
        return field.reshape(TOKEN_COUNT, HEAD_COUNT, HEAD_DIM).transpose(1, 0, 2)

    attn = lax.map(one_head, (heads_first(queries), heads_first(keys), heads_first(values), offsets))
    attn = attn.transpose(1, 0, 2).reshape(TOKEN_COUNT, D)
    return jnp.dot(attn, out_weight, preferred_element_type=jnp.float32).astype(jnp.bfloat16)
```

```python
import functools

import jax
import jax.numpy as jnp
from jax import lax
from jax.experimental import pallas as pl
from jax.experimental.pallas import tpu as pltpu
from jax.sharding import PartitionSpec as P

HEAD_DIM = 64
NEAR_DILATION = 8
FAR_DILATION = 16
SEGMENT = 8
ROWS = 1024
NEAR_ROWS = ROWS // NEAR_DILATION
FAR_ROWS = ROWS // FAR_DILATION
PICKED = NEAR_ROWS + FAR_ROWS
SENT_ROWS = PICKED + PICKED // 2
PAIR = 2 * HEAD_DIM
NEG = -1e30
SCALE = HEAD_DIM ** -0.5
BF16 = jnp.bfloat16
F32 = jnp.float32
ROW_BLOCK = 256


def lanes(shape):
    return lax.broadcasted_iota(jnp.int32, shape, 1)


def one_hot(offset_near, offset_far):
    row = lax.broadcasted_iota(jnp.int32, (PICKED, ROWS), 0)
    col = lax.broadcasted_iota(jnp.int32, (PICKED, ROWS), 1)
    at = jnp.where(
        row < NEAR_ROWS,
        row * NEAR_DILATION + offset_near,
        (row - NEAR_ROWS) * FAR_DILATION + offset_far,
    )
    return jnp.where(col == at, 1.0, 0.0).astype(BF16)


def pick_kernel(offsets_ref, q_ref, k_ref, v_ref, out_ref):
    pair = pl.program_id(0)
    for side in range(2):
        head = 2 * pair + side
        chosen = one_hot(offsets_ref[head, 0], offsets_ref[head, 1])
        q = jnp.dot(chosen, q_ref[...], preferred_element_type=F32)
        k = jnp.dot(chosen, k_ref[...], preferred_element_type=F32)
        v = jnp.dot(chosen, v_ref[...], preferred_element_type=F32)
        low = lanes((PICKED, PAIR)) < HEAD_DIM
        if side == 0:
            kv = jnp.where(low, k, pltpu.roll(v, HEAD_DIM, 1))
        else:
            kv = jnp.where(low, pltpu.roll(k, HEAD_DIM, 1), v)
        other = pltpu.roll(q, HEAD_DIM, 1)
        q_low, q_high = (q, other) if side == 0 else (other, q)
        q_packed = []
        for start, count in ((0, NEAR_ROWS), (NEAR_ROWS, FAR_ROWS)):
            half = count // 2
            q_packed.append(
                jnp.where(
                    lanes((half, PAIR)) < HEAD_DIM,
                    q_low[start : start + half],
                    q_high[start + half : start + count],
                )
            )
        out_ref[side, 0:PICKED, :] = kv.astype(BF16)
        out_ref[side, PICKED:SENT_ROWS, :] = (jnp.concatenate(q_packed, 0) * SCALE).astype(BF16)


def pick(queries, keys, values, offsets):
    heads = queries.shape[1] // HEAD_DIM
    pair_spec = pl.BlockSpec((ROWS, PAIR), lambda i: (0, i))
    return pl.pallas_call(
        pick_kernel,
        grid=(heads // 2,),
        in_specs=[pl.BlockSpec(memory_space=pltpu.SMEM)] + [pair_spec] * 3,
        out_specs=pl.BlockSpec((2, SENT_ROWS, PAIR), lambda i: (i, 0, 0)),
        out_shape=jax.ShapeDtypeStruct((heads, SENT_ROWS, PAIR), BF16),
        compiler_params=pltpu.CompilerParams(vmem_limit_bytes=32 * 1024 * 1024),
        cost_estimate=pl.CostEstimate(flops=10**9, bytes_accessed=4 * 10**6, transcendentals=0),
        name="pick_rows",
    )(offsets, queries, keys, values)


def contract_lanes(a, b):
    return lax.dot_general(a, b, (((1,), (1,)), ((), ())), preferred_element_type=F32)


def with_ones(v):
    return jnp.concatenate([v, jnp.ones_like(v)], 1)


def softmax_sum(scores, values):
    peak = functools.reduce(jnp.maximum, [jnp.max(s, axis=1, keepdims=True) for s in scores])
    acc = None
    for s, v in zip(scores, values):
        part = jnp.dot(jnp.exp(s - peak).astype(BF16), v, preferred_element_type=F32)
        acc = part if acc is None else acc + part
    total = acc[:, PAIR:]
    return acc[:, :PAIR] / total, peak + jnp.log(total)


def local_kernel(q_ref, k_ref, v_ref, out_ref, lse_ref):
    keys = k_ref[...]
    values = with_ones(v_ref[...])
    low = lanes((ROW_BLOCK, PAIR)) < HEAD_DIM
    zero = jnp.zeros((), BF16)

    def step(i, carry):
        rows = pl.ds(pl.multiple_of(i * ROW_BLOCK, ROW_BLOCK), ROW_BLOCK)
        q = q_ref[rows, :] * jnp.asarray(SCALE, BF16)
        both = [
            softmax_sum([contract_lanes(jnp.where(mine, q, zero), keys)], [values])
            for mine in (low, jnp.logical_not(low))
        ]
        out_ref[rows, :] = jnp.where(low, both[0][0], both[1][0]).astype(BF16)
        lse_ref[rows, :] = jnp.where(low, both[0][1], both[1][1])
        return carry

    lax.fori_loop(0, ROWS // ROW_BLOCK, step, 0)


def local_attention(queries, keys, values):
    pairs = queries.shape[1] // PAIR
    spec = pl.BlockSpec((ROWS, PAIR), lambda i: (0, i))
    return pl.pallas_call(
        local_kernel,
        grid=(pairs,),
        in_specs=[spec] * 3,
        out_specs=[spec] * 2,
        out_shape=[
            jax.ShapeDtypeStruct(queries.shape, BF16),
            jax.ShapeDtypeStruct(queries.shape, F32),
        ],
        compiler_params=pltpu.CompilerParams(vmem_limit_bytes=40 * 1024 * 1024),
        cost_estimate=pl.CostEstimate(
            flops=16 * 10**9, bytes_accessed=8 * 10**6, transcendentals=8 * 2**20
        ),
        name="local_attention",
    )(queries, keys, values)


def unpack_queries(packed):
    low = lanes(packed.shape) < HEAD_DIM
    wide = packed.astype(F32)
    top = jnp.where(low, wide, 0.0).astype(BF16)
    bottom = jnp.where(low, pltpu.roll(wide, HEAD_DIM, 1), 0.0).astype(BF16)
    return top, bottom


def result_rows(out, lse):
    high = lse.astype(BF16)
    rest = (lse - high.astype(F32)).astype(BF16)
    lane = lanes(out.shape)
    moved = pltpu.roll(out, HEAD_DIM, 1)
    stats = jnp.where(lane < HEAD_DIM + HEAD_DIM // 2, high.astype(F32), rest.astype(F32))
    return jnp.where(lane < HEAD_DIM, moved, stats).astype(BF16)


def spread_kernel(sent_ref, far0_ref, far1_ref, far2_ref, far3_ref, out_ref):
    near_kv = jnp.concatenate([sent_ref[i, 0:NEAR_ROWS, :] for i in range(SEGMENT)], 0)
    near_values = with_ones(near_kv)
    far = [r[...] for r in (far0_ref, far1_ref, far2_ref, far3_ref)]
    far_values = [with_ones(f) for f in far]

    def near_step(i, carry):
        packed = jnp.concatenate(
            [sent_ref[2 * i + j, PICKED : PICKED + NEAR_ROWS // 2, :] for j in range(2)], 0
        )
        half = NEAR_ROWS // 2
        top, bottom = unpack_queries(packed)
        q = jnp.concatenate([top, bottom], 0)
        out, lse = softmax_sum([contract_lanes(q, near_kv)], [near_values])
        res = result_rows(out, lse)
        for j in range(2):
            out_ref[2 * i + j, 0:half, :] = res[j * half : (j + 1) * half]
            out_ref[2 * i + j, half:NEAR_ROWS, :] = res[(2 + j) * half : (3 + j) * half]
        return carry

    lax.fori_loop(0, SEGMENT // 2, near_step, 0)

    def far_step(i, carry):
        half = FAR_ROWS // 2
        packed = jnp.concatenate(
            [sent_ref[4 * i + j, PICKED + NEAR_ROWS // 2 : SENT_ROWS, :] for j in range(4)], 0
        )
        top, bottom = unpack_queries(packed)
        q = jnp.concatenate([top, bottom], 0)
        out, lse = softmax_sum([contract_lanes(q, f) for f in far], far_values)
        res = result_rows(out, lse)
        for j in range(4):
            out_ref[4 * i + j, NEAR_ROWS : NEAR_ROWS + half, :] = res[j * half : (j + 1) * half]
            out_ref[4 * i + j, NEAR_ROWS + half : PICKED, :] = res[(4 + j) * half : (5 + j) * half]
        return carry

    lax.fori_loop(0, SEGMENT // 4, far_step, 0)


def spread_attention(sent, far):
    return pl.pallas_call(
        spread_kernel,
        in_specs=[pl.BlockSpec(memory_space=pltpu.VMEM)] * 5,
        out_specs=pl.BlockSpec(memory_space=pltpu.VMEM),
        out_shape=jax.ShapeDtypeStruct((SEGMENT, PICKED, PAIR), BF16),
        compiler_params=pltpu.CompilerParams(vmem_limit_bytes=40 * 1024 * 1024),
        cost_estimate=pl.CostEstimate(
            flops=6 * 10**9, bytes_accessed=2 * 10**6, transcendentals=3 * 2**20
        ),
        name="spread_attention",
    )(sent, *far)


def combine_kernel(offsets_ref, out_ref, lse_ref, back_ref, attn_ref):
    pair = pl.program_id(0)
    low_rows = lanes((ROWS, PAIR)) < HEAD_DIM
    position = lax.broadcasted_iota(jnp.int32, (ROWS, PAIR), 0)
    outs = [out_ref[...].astype(F32)]
    lses = [lse_ref[...]]
    for which, (start, count, dilation) in enumerate(
        ((0, NEAR_ROWS, NEAR_DILATION), (NEAR_ROWS, FAR_ROWS, FAR_DILATION))
    ):
        offset = [offsets_ref[2 * pair + side, which] for side in range(2)]
        row = lax.broadcasted_iota(jnp.int32, (ROWS, 2 * count), 0)
        col = lax.broadcasted_iota(jnp.int32, (ROWS, 2 * count), 1)
        at = jnp.where(
            col < count, col * dilation + offset[0], (col - count) * dilation + offset[1]
        )
        placed = jnp.where(row == at, 1.0, 0.0).astype(BF16)
        low = lanes((count, PAIR)) < HEAD_DIM
        first = back_ref[0, start : start + count, :].astype(F32)
        second = back_ref[1, start : start + count, :].astype(F32)
        high_first, rest_first = first[:, 64:65], first[:, 96:97]
        high_second, rest_second = second[:, 64:65], second[:, 96:97]
        zero = jnp.zeros((count, PAIR), F32)
        top = jnp.concatenate(
            [
                jnp.where(low, first, zero),
                jnp.where(low, high_first, zero),
                jnp.where(low, rest_first, zero),
            ],
            1,
        )
        bottom = jnp.concatenate(
            [
                jnp.where(low, zero, pltpu.roll(second, HEAD_DIM, 1)),
                jnp.where(low, zero, high_second),
                jnp.where(low, zero, rest_second),
            ],
            1,
        )
        wide = jnp.dot(
            placed, jnp.concatenate([top, bottom], 0).astype(BF16), preferred_element_type=F32
        )
        here = jnp.where(low_rows, offset[0], offset[1])
        hit = lax.rem(position, dilation) == here
        outs.append(wide[:, :PAIR])
        lses.append(jnp.where(hit, wide[:, PAIR : 2 * PAIR] + wide[:, 2 * PAIR :], NEG))
    top = jnp.maximum(jnp.maximum(lses[0], lses[1]), lses[2])
    numer, denom = 0.0, 0.0
    for out, lse in zip(outs, lses):
        weight = jnp.exp(lse - top)
        numer = numer + weight * out
        denom = denom + weight
    attn_ref[...] = (numer / denom).astype(BF16)


def combine(offsets, out, lse, back):
    pairs = out.shape[1] // PAIR
    spec = pl.BlockSpec((ROWS, PAIR), lambda i: (0, i))
    return pl.pallas_call(
        combine_kernel,
        grid=(pairs,),
        in_specs=[
            pl.BlockSpec(memory_space=pltpu.SMEM),
            spec,
            spec,
            pl.BlockSpec((2, PICKED, PAIR), lambda i: (i, 0, 0)),
        ],
        out_specs=spec,
        out_shape=jax.ShapeDtypeStruct(out.shape, BF16),
        compiler_params=pltpu.CompilerParams(vmem_limit_bytes=40 * 1024 * 1024),
        cost_estimate=pl.CostEstimate(flops=10**9, bytes_accessed=6 * 10**6, transcendentals=0),
        name="combine_patterns",
    )(offsets, out, lse, back)


def swap(shard, axis, bits):
    return lax.ppermute(shard, axis, [(i, i ^ bits) for i in range(lax.axis_size(axis))])


def local(queries, keys, values, offsets, out_weight):
    heads = queries.shape[1] // HEAD_DIM
    place = lax.axis_index("tp")
    upper, core = place // 2, place % 2
    mine = lax.dynamic_slice_in_dim(offsets, place * heads, heads, 0)
    mine = jnp.stack([mine[:, 0] % NEAR_DILATION, mine[:, 1] % FAR_DILATION], 1)

    picked = pick(queries, keys, values, mine)
    segments = [
        [s * SEGMENT + i for i in range(SEGMENT)]
        for s in range(lax.axis_size("ctx") // SEGMENT)
    ]
    sent = lax.all_to_all(picked, "ctx", 0, 0, axis_index_groups=segments, tiled=True)
    out, lse = local_attention(queries, keys, values)

    far_kv = sent[:, NEAR_ROWS:PICKED, :].reshape(SEGMENT * FAR_ROWS, PAIR)
    far_kv = jnp.concatenate([far_kv, swap(far_kv, "ctx", 8)], 0)
    far = [far_kv] + [swap(far_kv, "ctx", 16 * i) for i in (1, 2, 3)]

    back = spread_attention(sent, far)
    back = lax.all_to_all(back, "ctx", 0, 0, axis_index_groups=segments, tiled=True)
    attn = combine(mine, out, lse, back)

    half = ROWS // 2
    own = lax.dynamic_slice_in_dim(attn, upper * half, half, 0)
    away = lax.dynamic_slice_in_dim(attn, (1 - upper) * half, half, 0)
    came = swap(away, "tp", 2)
    n_tp = lax.axis_size("tp")
    n_ctx = lax.axis_size("ctx")
    other = [
        (c * n_tp + t, (c ^ 1) * n_tp + (t ^ 2)) for c in range(n_ctx) for t in range(n_tp)
    ]
    cut = out_weight.shape[0] // 2
    weight_there = jnp.concatenate(
        [
            swap(out_weight[:cut], "tp", 2),
            lax.ppermute(out_weight[cut:], ("ctx", "tp"), other),
        ],
        0,
    )
    share = jnp.dot(own, out_weight, preferred_element_type=F32) + jnp.dot(
        came, weight_there, preferred_element_type=F32
    )
    quarter = half // 2
    keep = lax.dynamic_slice_in_dim(share, core * quarter, quarter, 0)
    give = lax.dynamic_slice_in_dim(share, (1 - core) * quarter, quarter, 0).astype(BF16)
    return (keep + swap(give, "tp", 1).astype(F32)).astype(BF16)


def solution(mesh):
    return jax.shard_map(
        local,
        mesh=mesh,
        in_specs=(P("ctx", "tp"), P("ctx", "tp"), P("ctx", "tp"), P(), P("tp", None)),
        out_specs=P(("ctx", "tp"), None),
        check_vma=False,
    )
```

```python
import functools

import jax
import jax.numpy as jnp
from jax import lax
from jax.experimental import pallas as pl
from jax.experimental.pallas import tpu as pltpu
from jax.sharding import PartitionSpec as P

HEAD_DIM = 64
NEAR_DILATION = 8
FAR_DILATION = 16
SEGMENT = 8
ROWS = 1024
NEAR_ROWS = ROWS // NEAR_DILATION
FAR_ROWS = ROWS // FAR_DILATION
QUARTER = ROWS // 4
QUARTER_PICKED = QUARTER // NEAR_DILATION + QUARTER // FAR_DILATION
PICKED = NEAR_ROWS + FAR_ROWS
SENT_ROWS = PICKED + PICKED // 2
PAIR = 2 * HEAD_DIM
NEG = -1e30
SCALE = HEAD_DIM ** -0.5
BF16 = jnp.bfloat16
F32 = jnp.float32
ROW_BLOCK = 128
VMEM_BYTES = 56 * 1024 * 1024
LESS_VMEM_BYTES = 20 * 1024 * 1024
SMALL = pl.CostEstimate(flops=1000, bytes_accessed=1000, transcendentals=0)


def lanes(shape):
    return lax.broadcasted_iota(jnp.int32, shape, 1)


def one_hot(offset_near, offset_far):
    row = lax.broadcasted_iota(jnp.int32, (QUARTER_PICKED, QUARTER), 0)
    col = lax.broadcasted_iota(jnp.int32, (QUARTER_PICKED, QUARTER), 1)
    count = QUARTER // NEAR_DILATION
    at = jnp.where(
        row < count,
        row * NEAR_DILATION + offset_near,
        (row - count) * FAR_DILATION + offset_far,
    )
    return jnp.where(col == at, 1.0, 0.0).astype(BF16)


def pick_kernel(offsets_ref, q_ref, k_ref, v_ref, out_ref):
    pair = pl.program_id(0)
    chosen = jnp.concatenate(
        [one_hot(offsets_ref[2 * pair + i, 0], offsets_ref[2 * pair + i, 1]) for i in range(2)], 0
    )
    split = QUARTER // NEAR_DILATION
    found = []
    for i in range(ROWS // QUARTER):
        block = slice(i * QUARTER, (i + 1) * QUARTER)
        fields = jnp.concatenate([q_ref[block, :], k_ref[block, :], v_ref[block, :]], 1)
        found.append(jnp.dot(chosen, fields, preferred_element_type=F32))
    low = lanes((PICKED, PAIR)) < HEAD_DIM
    for side in range(2):
        base = side * QUARTER_PICKED
        part = jnp.concatenate(
            [f[base : base + split] for f in found]
            + [f[base + split : base + QUARTER_PICKED] for f in found],
            0,
        )
        q, k, v = (part[:, i * PAIR : (i + 1) * PAIR] for i in range(3))
        if side == 0:
            kv = jnp.where(low, k, pltpu.roll(v, HEAD_DIM, 1))
        else:
            kv = jnp.where(low, pltpu.roll(k, HEAD_DIM, 1), v)
        other = pltpu.roll(q, HEAD_DIM, 1)
        q_low, q_high = (q, other) if side == 0 else (other, q)
        q_packed = []
        for start, count in ((0, NEAR_ROWS), (NEAR_ROWS, FAR_ROWS)):
            half = count // 2
            q_packed.append(
                jnp.where(
                    lanes((half, PAIR)) < HEAD_DIM,
                    q_low[start : start + half],
                    q_high[start + half : start + count],
                )
            )
        out_ref[side, 0:PICKED, :] = kv.astype(BF16)
        out_ref[side, PICKED:SENT_ROWS, :] = (jnp.concatenate(q_packed, 0) * SCALE).astype(BF16)


def pick(queries, keys, values, offsets):
    heads = queries.shape[1] // HEAD_DIM
    pair_spec = pl.BlockSpec((ROWS, PAIR), lambda i: (0, i))
    return pl.pallas_call(
        pick_kernel,
        grid=(heads // 2,),
        in_specs=[pl.BlockSpec(memory_space=pltpu.SMEM)] + [pair_spec] * 3,
        out_specs=pl.BlockSpec((2, SENT_ROWS, PAIR), lambda i: (i, 0, 0)),
        out_shape=jax.ShapeDtypeStruct((heads, SENT_ROWS, PAIR), BF16),
        compiler_params=pltpu.CompilerParams(vmem_limit_bytes=VMEM_BYTES),
        cost_estimate=SMALL,
        name="pick_rows",
    )(offsets, queries, keys, values)


def contract_lanes(a, b):
    return lax.dot_general(a, b, (((1,), (1,)), ((), ())), preferred_element_type=F32)


def with_ones(v):
    return jnp.concatenate([v, jnp.ones_like(v)], 1)


def softmax_sum(scores, values):
    peak = functools.reduce(jnp.maximum, [jnp.max(s, axis=1, keepdims=True) for s in scores])
    acc = None
    for s, v in zip(scores, values):
        part = jnp.dot(jnp.exp(s - peak).astype(BF16), v, preferred_element_type=F32)
        acc = part if acc is None else acc + part
    total = acc[:, PAIR:]
    return acc[:, :PAIR] / total, peak + jnp.log(total)


def local_kernel(q_ref, k_ref, v_ref, out_ref, lse_ref):
    keys = k_ref[...]
    values = with_ones(v_ref[...])
    low = lanes((ROW_BLOCK, PAIR)) < HEAD_DIM
    zero = jnp.zeros((), BF16)

    for i in range(ROWS // ROW_BLOCK):
        rows = pl.ds(i * ROW_BLOCK, ROW_BLOCK)
        q = q_ref[rows, :] * jnp.asarray(SCALE, BF16)
        both = [
            softmax_sum([contract_lanes(jnp.where(mine, q, zero), keys)], [values])
            for mine in (low, jnp.logical_not(low))
        ]
        out_ref[rows, :] = jnp.where(low, both[0][0], both[1][0]).astype(BF16)
        lse_ref[rows, :] = jnp.where(low, both[0][1], both[1][1])


def local_attention(queries, keys, values, first, count):
    spec = pl.BlockSpec((ROWS, PAIR), lambda i: (0, i + first))
    out_spec = pl.BlockSpec((ROWS, PAIR), lambda i: (0, i))
    return pl.pallas_call(
        local_kernel,
        grid=(count,),
        in_specs=[spec] * 3,
        out_specs=[out_spec] * 2,
        out_shape=[
            jax.ShapeDtypeStruct((ROWS, count * PAIR), BF16),
            jax.ShapeDtypeStruct((ROWS, count * PAIR), F32),
        ],
        compiler_params=pltpu.CompilerParams(vmem_limit_bytes=VMEM_BYTES),
        cost_estimate=SMALL,
        name="local_attention",
    )(queries, keys, values)


def unpack_queries(packed):
    low = lanes(packed.shape) < HEAD_DIM
    wide = packed.astype(F32)
    top = jnp.where(low, wide, 0.0).astype(BF16)
    bottom = jnp.where(low, pltpu.roll(wide, HEAD_DIM, 1), 0.0).astype(BF16)
    return top, bottom


def result_rows(out, lse):
    high = lse.astype(BF16)
    rest = (lse - high.astype(F32)).astype(BF16)
    lane = lanes(out.shape)
    moved = pltpu.roll(out, HEAD_DIM, 1)
    stats = jnp.where(lane < HEAD_DIM + HEAD_DIM // 2, high.astype(F32), rest.astype(F32))
    return jnp.where(lane < HEAD_DIM, moved, stats).astype(BF16)


def near_kernel(sent_ref, out_ref):
    near_kv = jnp.concatenate([sent_ref[i, 0:NEAR_ROWS, :] for i in range(SEGMENT)], 0)
    near_values = with_ones(near_kv)
    half = NEAR_ROWS // 2
    for i in range(SEGMENT):
        q = jnp.concatenate(unpack_queries(sent_ref[i, PICKED : PICKED + half, :]), 0)
        out_ref[i] = result_rows(*softmax_sum([contract_lanes(q, near_kv)], [near_values]))


def far_kernel(sent_ref, far0_ref, far1_ref, far2_ref, far3_ref, out_ref):
    far = [r[...] for r in (far0_ref, far1_ref, far2_ref, far3_ref)]
    far_values = [with_ones(f) for f in far]
    half = FAR_ROWS // 2
    for i in range(SEGMENT // 2):
        packed = jnp.concatenate(
            [sent_ref[2 * i + j, SENT_ROWS - half : SENT_ROWS, :] for j in range(2)], 0
        )
        q = jnp.concatenate(unpack_queries(packed), 0)
        res = result_rows(*softmax_sum([contract_lanes(q, f) for f in far], far_values))
        for j in range(2):
            out_ref[2 * i + j, 0:half, :] = res[j * half : (j + 1) * half]
            out_ref[2 * i + j, half:FAR_ROWS, :] = res[(2 + j) * half : (3 + j) * half]


def near_attention(sent):
    return pl.pallas_call(
        near_kernel,
        in_specs=[pl.BlockSpec(memory_space=pltpu.VMEM)],
        out_specs=pl.BlockSpec(memory_space=pltpu.VMEM),
        out_shape=jax.ShapeDtypeStruct((SEGMENT, NEAR_ROWS, PAIR), BF16),
        compiler_params=pltpu.CompilerParams(vmem_limit_bytes=LESS_VMEM_BYTES),
        cost_estimate=SMALL,
        name="near_attention",
    )(sent)


def far_attention(sent, far):
    return pl.pallas_call(
        far_kernel,
        in_specs=[pl.BlockSpec(memory_space=pltpu.VMEM)] * 5,
        out_specs=pl.BlockSpec(memory_space=pltpu.VMEM),
        out_shape=jax.ShapeDtypeStruct((SEGMENT, FAR_ROWS, PAIR), BF16),
        compiler_params=pltpu.CompilerParams(vmem_limit_bytes=LESS_VMEM_BYTES),
        cost_estimate=SMALL,
        name="far_attention",
    )(sent, *far)


def combine_kernel(quarter_ref, offsets_ref, out_ref, lse_ref, out2_ref, lse2_ref, near_ref, far_ref, attn_ref):
    quarter = quarter_ref[0]
    low_rows = lanes((QUARTER, PAIR)) < HEAD_DIM
    position = lax.broadcasted_iota(jnp.int32, (QUARTER, PAIR), 0) + quarter * QUARTER
    early = out_ref.shape[1] // PAIR
    for pair in range(attn_ref.shape[1] // PAIR):
        columns = slice(pair * PAIR, (pair + 1) * PAIR)
        if pair < early:
            outs, lses = [out_ref[:, columns].astype(F32)], [lse_ref[:, columns]]
        else:
            late = slice((pair - early) * PAIR, (pair - early + 1) * PAIR)
            outs, lses = [out2_ref[:, late].astype(F32)], [lse2_ref[:, late]]
        for which, (back_ref, dilation) in enumerate(
            ((near_ref, NEAR_DILATION), (far_ref, FAR_DILATION))
        ):
            count = QUARTER // dilation
            rows = pl.ds(pl.multiple_of(quarter * count, count), count)
            offset = [offsets_ref[2 * pair + side, which] for side in range(2)]
            row = lax.broadcasted_iota(jnp.int32, (QUARTER, 2 * count), 0)
            col = lax.broadcasted_iota(jnp.int32, (QUARTER, 2 * count), 1)
            at = jnp.where(
                col < count, col * dilation + offset[0], (col - count) * dilation + offset[1]
            )
            placed = jnp.where(row == at, 1.0, 0.0).astype(BF16)
            low = lanes((count, PAIR)) < HEAD_DIM
            first = back_ref[2 * pair, rows, :].astype(F32)
            second = back_ref[2 * pair + 1, rows, :].astype(F32)
            zero = jnp.zeros((count, PAIR), F32)
            top = jnp.concatenate(
                [
                    jnp.where(low, first, zero),
                    jnp.where(low, first[:, 64:65], zero),
                    jnp.where(low, first[:, 96:97], zero),
                ],
                1,
            )
            bottom = jnp.concatenate(
                [
                    jnp.where(low, zero, pltpu.roll(second, HEAD_DIM, 1)),
                    jnp.where(low, zero, second[:, 64:65]),
                    jnp.where(low, zero, second[:, 96:97]),
                ],
                1,
            )
            wide = jnp.dot(
                placed, jnp.concatenate([top, bottom], 0).astype(BF16), preferred_element_type=F32
            )
            here = jnp.where(low_rows, offset[0], offset[1])
            hit = (position & (dilation - 1)) == here
            outs.append(wide[:, :PAIR])
            lses.append(jnp.where(hit, wide[:, PAIR : 2 * PAIR] + wide[:, 2 * PAIR :], NEG))
        peak = jnp.maximum(jnp.maximum(lses[0], lses[1]), lses[2])
        numer, denom = 0.0, 0.0
        for out, lse in zip(outs, lses):
            weight = jnp.exp(lse - peak)
            numer = numer + weight * out
            denom = denom + weight
        attn_ref[:, columns] = (numer / denom).astype(BF16)


def combine(quarter, offsets, local_parts, near, far):
    blocks = [
        pl.BlockSpec((QUARTER, part.shape[1]), lambda i, quarter: (quarter[0], 0))
        for part in local_parts
    ]
    whole = [pl.BlockSpec(memory_space=pltpu.VMEM)] * 2
    width = sum(part.shape[1] for part in local_parts[::2])
    return pl.pallas_call(
        combine_kernel,
        grid_spec=pltpu.PrefetchScalarGridSpec(
            num_scalar_prefetch=1,
            grid=(1,),
            in_specs=[pl.BlockSpec(memory_space=pltpu.SMEM)] + blocks + whole,
            out_specs=pl.BlockSpec((QUARTER, width), lambda i, quarter: (0, 0)),
        ),
        out_shape=jax.ShapeDtypeStruct((QUARTER, width), BF16),
        compiler_params=pltpu.CompilerParams(vmem_limit_bytes=LESS_VMEM_BYTES),
        cost_estimate=SMALL,
        name="combine_patterns",
    )(quarter.reshape(1), offsets, *local_parts, near, far)


def project_kernel(has_base, *refs):
    out_ref = refs[-1]
    base_ref = refs[0] if has_base else None
    terms = refs[1:-1] if has_base else refs[:-1]
    width = 512
    for start in range(0, out_ref.shape[1], width):
        columns = slice(start, start + width)
        total = base_ref[:, columns] if has_base else None
        for rows_ref, first, weight_ref in zip(terms[0::2], (0, 256) * 4, terms[1::2]):
            rows = rows_ref[...]
            depth = weight_ref.shape[0]
            if depth < rows.shape[1]:
                rows = rows[:, first : first + depth]
            part = jnp.dot(rows, weight_ref[:, columns], preferred_element_type=F32)
            total = part if total is None else total + part
        out_ref[:, columns] = total.astype(out_ref.dtype)


def project(base, terms, dtype):
    operands = ([] if base is None else [base]) + [x for term in terms for x in term]
    width = terms[0][1].shape[1]
    return pl.pallas_call(
        functools.partial(project_kernel, base is not None),
        in_specs=[pl.BlockSpec(memory_space=pltpu.VMEM)] * len(operands),
        out_specs=pl.BlockSpec(memory_space=pltpu.VMEM),
        out_shape=jax.ShapeDtypeStruct((QUARTER, width), dtype),
        compiler_params=pltpu.CompilerParams(vmem_limit_bytes=LESS_VMEM_BYTES),
        cost_estimate=SMALL,
        name="project",
    )(*operands)


def swap(shard, axis, bits):
    return lax.ppermute(shard, axis, [(i, i ^ bits) for i in range(lax.axis_size(axis))])


def local(queries, keys, values, offsets, out_weight):
    heads = queries.shape[1] // HEAD_DIM
    place = lax.axis_index("tp")
    mine = lax.dynamic_slice_in_dim(offsets, place * heads, heads, 0)
    mine = jnp.stack([mine[:, 0] % NEAR_DILATION, mine[:, 1] % FAR_DILATION], 1)
    n_tp, n_ctx = lax.axis_size("tp"), lax.axis_size("ctx")

    picked = pick(queries, keys, values, mine)
    picked, sent_weight = lax.optimization_barrier((picked, out_weight))
    segments = [[s * SEGMENT + i for i in range(SEGMENT)] for s in range(n_ctx // SEGMENT)]
    sent = lax.all_to_all(picked, "ctx", 0, 0, axis_index_groups=segments, tiled=True)
    other = [(c * n_tp + t, (c ^ 1) * n_tp + (t ^ 2)) for c in range(n_ctx) for t in range(n_tp)]
    cut = out_weight.shape[0] // 2
    weight_2 = [
        swap(sent_weight[:cut], "tp", 2),
        lax.ppermute(sent_weight[cut:], ("ctx", "tp"), other),
    ]
    weight_1 = swap(sent_weight, "tp", 1)
    early = local_attention(queries, keys, values, 0, 3)
    sent, early, weight_1 = lax.optimization_barrier((sent, early, weight_1))

    far_kv = sent[:, NEAR_ROWS:PICKED, :].reshape(SEGMENT * FAR_ROWS, PAIR)
    far_kv = jnp.concatenate([far_kv, swap(far_kv, "ctx", 8)], 0)
    near_back = near_attention(sent)
    far_kv, near_back, queries = lax.optimization_barrier((far_kv, near_back, queries))
    far = [far_kv] + [swap(far_kv, "ctx", 16 * i) for i in (1, 2, 3)]
    late = local_attention(queries, keys, values, 3, 1)
    far, late, weight_2 = lax.optimization_barrier((far, late, weight_2))
    weight_3 = [swap(w, "tp", 1) for w in weight_2]

    back = jnp.concatenate([near_back, far_attention(sent, far)], 1)
    back = lax.all_to_all(back, "ctx", 0, 0, axis_index_groups=segments, tiled=True)
    near_rows, far_rows = back[:, :NEAR_ROWS], back[:, NEAR_ROWS:]
    local_parts = [*early, *late]
    away = [combine(place ^ i, mine, local_parts, near_rows, far_rows) for i in (3, 2)]
    came_3, came_2 = (swap(rows, "tp", i) for rows, i in zip(away, (3, 2)))
    near_rows, far_rows, _ = lax.optimization_barrier((near_rows, far_rows, away))
    came_1 = swap(combine(place ^ 1, mine, local_parts, near_rows, far_rows), "tp", 1)
    own = combine(place, mine, local_parts, near_rows, far_rows)
    base = project(None, [(own, out_weight), (came_1, weight_1)], F32)
    terms = [(came_2, w) for w in weight_2] + [(came_3, w) for w in weight_3]
    return project(base, terms, BF16)


def solution(mesh):
    return jax.shard_map(
        local,
        mesh=mesh,
        in_specs=(P("ctx", "tp"), P("ctx", "tp"), P("ctx", "tp"), P(), P("tp", None)),
        out_specs=P(("ctx", "tp"), None),
        check_vma=False,
    )
```

```python
import functools

import jax
import jax.numpy as jnp
from jax import lax
from jax.experimental import pallas as pl
from jax.experimental.pallas import tpu as pltpu
from jax.sharding import PartitionSpec as P

HEAD_DIM = 64
NEAR_DILATION = 8
FAR_DILATION = 16
SEGMENT = 8
ROWS = 1024
NEAR_ROWS = ROWS // NEAR_DILATION
FAR_ROWS = ROWS // FAR_DILATION
QUARTER = ROWS // 4
NEAR_PART = QUARTER // NEAR_DILATION
FAR_PART = QUARTER // FAR_DILATION
QUARTER_PICKED = NEAR_PART + FAR_PART
PICKED = NEAR_ROWS + FAR_ROWS
SENT_ROWS = PICKED + PICKED // 2
PAIR = 2 * HEAD_DIM
NEG = -1e30
SCALE = HEAD_DIM ** -0.5
BF16 = jnp.bfloat16
F32 = jnp.float32
ROW_BLOCK = 128
VMEM_BYTES = 56 * 1024 * 1024
LESS_VMEM_BYTES = 20 * 1024 * 1024
SMALL = pl.CostEstimate(flops=1000, bytes_accessed=1000, transcendentals=0)


def lanes(shape):
    return lax.broadcasted_iota(jnp.int32, shape, 1)


def head_offsets(offsets_ref, head):
    near = lax.rem(offsets_ref[0, head], NEAR_DILATION)
    return near, lax.rem(offsets_ref[1, head], FAR_DILATION)


def one_hot(offset_near, offset_far):
    row = lax.broadcasted_iota(jnp.int32, (QUARTER_PICKED, QUARTER), 0)
    col = lax.broadcasted_iota(jnp.int32, (QUARTER_PICKED, QUARTER), 1)
    count = QUARTER // NEAR_DILATION
    at = jnp.where(
        row < count,
        row * NEAR_DILATION + offset_near,
        (row - count) * FAR_DILATION + offset_far,
    )
    return jnp.where(col == at, 1.0, 0.0).astype(BF16)


def pick_kernel(offsets_ref, q_ref, k_ref, v_ref, out_ref):
    heads = 2 * pl.num_programs(0)
    first = lax.axis_index("tp") * heads + 2 * pl.program_id(0)
    chosen = jnp.concatenate([one_hot(*head_offsets(offsets_ref, first + i)) for i in range(2)], 0)
    split = QUARTER // NEAR_DILATION
    found = []
    for i in range(ROWS // QUARTER):
        block = slice(i * QUARTER, (i + 1) * QUARTER)
        fields = jnp.concatenate([q_ref[block, :], k_ref[block, :], v_ref[block, :]], 1)
        found.append(jnp.dot(chosen, fields, preferred_element_type=F32))
    low = lanes((PICKED, PAIR)) < HEAD_DIM
    for side in range(2):
        base = side * QUARTER_PICKED
        part = jnp.concatenate(
            [f[base : base + split] for f in found]
            + [f[base + split : base + QUARTER_PICKED] for f in found],
            0,
        )
        q, k, v = (part[:, i * PAIR : (i + 1) * PAIR] for i in range(3))
        if side == 0:
            kv = jnp.where(low, k, pltpu.roll(v, HEAD_DIM, 1))
        else:
            kv = jnp.where(low, pltpu.roll(k, HEAD_DIM, 1), v)
        other = pltpu.roll(q, HEAD_DIM, 1)
        q_low, q_high = (q, other) if side == 0 else (other, q)
        q_packed = []
        for start, count in ((0, NEAR_ROWS), (NEAR_ROWS, FAR_ROWS)):
            half = count // 2
            q_packed.append(
                jnp.where(
                    lanes((half, PAIR)) < HEAD_DIM,
                    q_low[start : start + half],
                    q_high[start + half : start + count],
                )
            )
        out_ref[side, 0:PICKED, :] = kv.astype(BF16)
        out_ref[side, PICKED:SENT_ROWS, :] = (jnp.concatenate(q_packed, 0) * SCALE).astype(BF16)


def pick(queries, keys, values, offsets):
    heads = queries.shape[1] // HEAD_DIM
    pair_spec = pl.BlockSpec((ROWS, PAIR), lambda i: (0, i))
    return pl.pallas_call(
        pick_kernel,
        grid=(heads // 2,),
        in_specs=[pl.BlockSpec(memory_space=pltpu.SMEM)] + [pair_spec] * 3,
        out_specs=pl.BlockSpec((2, SENT_ROWS, PAIR), lambda i: (i, 0, 0)),
        out_shape=jax.ShapeDtypeStruct((heads, SENT_ROWS, PAIR), BF16),
        compiler_params=pltpu.CompilerParams(vmem_limit_bytes=VMEM_BYTES),
        cost_estimate=SMALL,
        name="pick_rows",
    )(offsets, queries, keys, values)


def contract_lanes(a, b):
    return lax.dot_general(a, b, (((1,), (1,)), ((), ())), preferred_element_type=F32)


def with_ones(v):
    return jnp.concatenate([v, jnp.ones_like(v)], 1)


def softmax_sum(scores, values):
    peak = functools.reduce(jnp.maximum, [jnp.max(s, axis=1, keepdims=True) for s in scores])
    acc = None
    for s, v in zip(scores, values):
        part = jnp.dot(jnp.exp(s - peak).astype(BF16), v, preferred_element_type=F32)
        acc = part if acc is None else acc + part
    total = acc[:, PAIR:]
    return acc[:, :PAIR] / total, peak + jnp.log(total)


def local_kernel(q_ref, k_ref, v_ref, pack_ref):
    pair = pl.program_id(0)
    keys = k_ref[...]
    values = with_ones(v_ref[...])
    low = lanes((ROW_BLOCK, PAIR)) < HEAD_DIM
    lane = lanes((ROW_BLOCK, PAIR))
    zero = jnp.zeros((), BF16)
    columns = pl.ds(pl.multiple_of(pair * PAIR, PAIR), PAIR)
    stats_at = pack_ref.shape[1] - PAIR
    for i in range(ROWS // ROW_BLOCK):
        rows = pl.ds(i * ROW_BLOCK, ROW_BLOCK)
        q = q_ref[rows, :] * jnp.asarray(SCALE, BF16)
        both = [
            softmax_sum([contract_lanes(jnp.where(mine, q, zero), keys)], [values])
            for mine in (low, jnp.logical_not(low))
        ]
        pack_ref[rows, columns] = jnp.where(low, both[0][0], both[1][0]).astype(BF16)
        lse = jnp.where((lane & 1) == 0, both[0][1], both[1][1])
        high = lse.astype(BF16)
        rest = (lse - high.astype(F32)).astype(BF16)
        stats = jnp.where(low, high.astype(F32), rest.astype(F32))
        held = pack_ref[rows, stats_at:].astype(F32)
        mine = (lane & (HEAD_DIM - 1)) // 2 == pair
        pack_ref[rows, stats_at:] = jnp.where(
            mine, stats, jnp.where(pair == 0, 0.0, held)
        ).astype(BF16)


def local_attention(queries, keys, values):
    spec = pl.BlockSpec((ROWS, PAIR), lambda i: (0, i))
    width = queries.shape[1] + PAIR
    return pl.pallas_call(
        local_kernel,
        grid=(queries.shape[1] // PAIR,),
        in_specs=[spec] * 3,
        out_specs=pl.BlockSpec((ROWS, width), lambda i: (0, 0)),
        out_shape=jax.ShapeDtypeStruct((ROWS, width), BF16),
        compiler_params=pltpu.CompilerParams(vmem_limit_bytes=VMEM_BYTES),
        cost_estimate=SMALL,
        name="local_attention",
    )(queries, keys, values)


def unpack_queries(packed):
    low = lanes(packed.shape) < HEAD_DIM
    wide = packed.astype(F32)
    top = jnp.where(low, wide, 0.0).astype(BF16)
    bottom = jnp.where(low, pltpu.roll(wide, HEAD_DIM, 1), 0.0).astype(BF16)
    return top, bottom


def result_rows(out, lse):
    high = lse.astype(BF16)
    rest = (lse - high.astype(F32)).astype(BF16)
    lane = lanes(out.shape)
    moved = pltpu.roll(out, HEAD_DIM, 1)
    stats = jnp.where(lane < HEAD_DIM + HEAD_DIM // 2, high.astype(F32), rest.astype(F32))
    return jnp.where(lane < HEAD_DIM, moved, stats).astype(BF16)


def near_kernel(sent_ref, out_ref):
    near_kv = jnp.concatenate([sent_ref[i, 0:NEAR_ROWS, :] for i in range(SEGMENT)], 0)
    near_values = with_ones(near_kv)
    half = NEAR_ROWS // 2
    for i in range(SEGMENT):
        q = jnp.concatenate(unpack_queries(sent_ref[i, PICKED : PICKED + half, :]), 0)
        res = result_rows(*softmax_sum([contract_lanes(q, near_kv)], [near_values]))
        for t in range(4):
            out_ref[t * SEGMENT + i] = res[t * NEAR_PART : (t + 1) * NEAR_PART]


def far_queries(sent_ref, i):
    half = FAR_ROWS // 2
    packed = jnp.concatenate(
        [sent_ref[2 * i + j, SENT_ROWS - half : SENT_ROWS, :] for j in range(2)], 0
    )
    return jnp.concatenate(unpack_queries(packed), 0)


def first_far_kernel(sent_ref, far0_ref, far1_ref, far2_ref, far3_ref, out_ref, lse_ref):
    far = [r[...] for r in (far0_ref, far1_ref, far2_ref, far3_ref)]
    far_values = [with_ones(f) for f in far]
    for i in range(SEGMENT // 2):
        q = far_queries(sent_ref, i)
        out, lse = softmax_sum([contract_lanes(q, f) for f in far], far_values)
        rows = slice(i * PAIR, (i + 1) * PAIR)
        out_ref[rows, :] = out
        lse_ref[rows, :] = lse


def second_far_kernel(
    sent_ref, near_ref, held_ref, held_lse_ref, far0_ref, far1_ref, far2_ref, far3_ref, out_ref
):
    far = [r[...] for r in (far0_ref, far1_ref, far2_ref, far3_ref)]
    far_values = [with_ones(f) for f in far]
    half = FAR_ROWS // 2
    out_ref[:, 0:NEAR_PART, :] = near_ref[...]
    for i in range(SEGMENT // 2):
        q = far_queries(sent_ref, i)
        out, lse = softmax_sum([contract_lanes(q, f) for f in far], far_values)
        rows = slice(i * PAIR, (i + 1) * PAIR)
        held, held_lse = held_ref[rows, :], held_lse_ref[rows, :]
        peak = jnp.maximum(lse, held_lse)
        new, old = jnp.exp(lse - peak), jnp.exp(held_lse - peak)
        both = new + old
        res = result_rows((new * out + old * held) / both, peak + jnp.log(both))
        for t in range(4):
            for j in range(2):
                at = ((t // 2) * 2 + j) * half + (t % 2) * FAR_PART
                out_ref[t * SEGMENT + 2 * i + j, NEAR_PART:, :] = res[at : at + FAR_PART]


def near_attention(sent):
    return pl.pallas_call(
        near_kernel,
        in_specs=[pl.BlockSpec(memory_space=pltpu.VMEM)],
        out_specs=pl.BlockSpec(memory_space=pltpu.VMEM),
        out_shape=jax.ShapeDtypeStruct((4 * SEGMENT, NEAR_PART, PAIR), BF16),
        compiler_params=pltpu.CompilerParams(vmem_limit_bytes=LESS_VMEM_BYTES),
        cost_estimate=SMALL,
        name="near_attention",
    )(sent)


def first_far_attention(sent, far):
    return pl.pallas_call(
        first_far_kernel,
        in_specs=[pl.BlockSpec(memory_space=pltpu.VMEM)] * 5,
        out_specs=[pl.BlockSpec(memory_space=pltpu.VMEM)] * 2,
        out_shape=[jax.ShapeDtypeStruct((SEGMENT * FAR_ROWS, PAIR), F32)] * 2,
        compiler_params=pltpu.CompilerParams(vmem_limit_bytes=LESS_VMEM_BYTES),
        cost_estimate=SMALL,
        name="first_far_attention",
    )(sent, *far)


def second_far_attention(sent, near_back, held, far):
    return pl.pallas_call(
        second_far_kernel,
        in_specs=[pl.BlockSpec(memory_space=pltpu.VMEM)] * 8,
        out_specs=pl.BlockSpec(memory_space=pltpu.VMEM),
        out_shape=jax.ShapeDtypeStruct((4 * SEGMENT, QUARTER_PICKED, PAIR), BF16),
        compiler_params=pltpu.CompilerParams(vmem_limit_bytes=LESS_VMEM_BYTES),
        cost_estimate=SMALL,
        name="second_far_attention",
    )(sent, near_back, *held, *far)


def combine_pair(offsets_ref, back_ref, head, out, lse, low_rows, position):
    outs, lses = [out], [lse]
    offsets = [head_offsets(offsets_ref, head + side) for side in range(2)]
    for which, (start, count, dilation) in enumerate(
        ((0, NEAR_PART, NEAR_DILATION), (NEAR_PART, FAR_PART, FAR_DILATION))
    ):
        offset = [o[which] for o in offsets]
        row = lax.broadcasted_iota(jnp.int32, (QUARTER, 2 * count), 0)
        col = lax.broadcasted_iota(jnp.int32, (QUARTER, 2 * count), 1)
        at = jnp.where(
            col < count, col * dilation + offset[0], (col - count) * dilation + offset[1]
        )
        placed = jnp.where(row == at, 1.0, 0.0).astype(BF16)
        low = lanes((count, PAIR)) < HEAD_DIM
        first = back_ref[head, start : start + count, :].astype(F32)
        second = back_ref[head + 1, start : start + count, :].astype(F32)
        zero = jnp.zeros((count, PAIR), F32)
        top = jnp.concatenate(
            [
                jnp.where(low, first, zero),
                jnp.where(low, first[:, 64:65], zero),
                jnp.where(low, first[:, 96:97], zero),
            ],
            1,
        )
        bottom = jnp.concatenate(
            [
                jnp.where(low, zero, pltpu.roll(second, HEAD_DIM, 1)),
                jnp.where(low, zero, second[:, 64:65]),
                jnp.where(low, zero, second[:, 96:97]),
            ],
            1,
        )
        wide = jnp.dot(
            placed, jnp.concatenate([top, bottom], 0).astype(BF16), preferred_element_type=F32
        )
        here = jnp.where(low_rows, offset[0], offset[1])
        hit = (position & (dilation - 1)) == here
        outs.append(wide[:, :PAIR])
        lses.append(jnp.where(hit, wide[:, PAIR : 2 * PAIR] + wide[:, 2 * PAIR :], NEG))
    peak = jnp.maximum(jnp.maximum(lses[0], lses[1]), lses[2])
    numer, denom = 0.0, 0.0
    for out, lse in zip(outs, lses):
        weight = jnp.exp(lse - peak)
        numer = numer + weight * out
        denom = denom + weight
    return (numer / denom).astype(BF16)


def finish_kernel(offsets_ref, pack_ref, back_ref, *refs):
    weight_refs, (total_ref, last_ref, held, sems) = refs[:-4], refs[-4:]
    depth = held.shape[1]
    copies = [
        pltpu.make_async_copy(weight, held.at[i], sems.at[i]) for i, weight in enumerate(weight_refs)
    ]
    for copy in copies:
        copy.start()
    place = lax.axis_index("tp")
    heads = depth // HEAD_DIM
    low_rows = lanes((QUARTER, PAIR)) < HEAD_DIM
    position = lax.broadcasted_iota(jnp.int32, (QUARTER, PAIR), 0)
    source = lax.broadcasted_iota(jnp.int32, (PAIR, depth), 0) & (HEAD_DIM - 1)
    widen = jnp.where(source == lanes((PAIR, depth)) // HEAD_DIM, 1.0, 0.0).astype(BF16)
    for i in range(4):
        who = place ^ i
        rows = pl.ds(pl.multiple_of(who * QUARTER, QUARTER), QUARTER)
        lse = jnp.dot(pack_ref[rows, depth:], widen, preferred_element_type=F32)
        attn = []
        for pair in range(depth // PAIR):
            columns = slice(pair * PAIR, (pair + 1) * PAIR)
            attn.append(
                combine_pair(
                    offsets_ref,
                    back_ref,
                    who * heads + 2 * pair,
                    pack_ref[rows, columns].astype(F32),
                    lse[:, columns],
                    low_rows,
                    position,
                )
            )
        attn = jnp.concatenate(attn, 1)
        if i == 3:
            last_ref[...] = attn
            continue
        copies[i].wait()
        for start in range(0, total_ref.shape[1], 512):
            columns = slice(start, start + 512)
            part = jnp.dot(attn, held[i, :, columns], preferred_element_type=F32)
            if i > 0:
                part = part + total_ref[:, columns]
            total_ref[:, columns] = part


def finish(offsets, pack, back, weights):
    depth, width = weights[0].shape
    vmem = pl.BlockSpec(memory_space=pltpu.VMEM)
    return pl.pallas_call(
        finish_kernel,
        in_specs=[pl.BlockSpec(memory_space=pltpu.SMEM), vmem, vmem]
        + [pl.BlockSpec(memory_space=pl.ANY)] * len(weights),
        out_specs=[vmem, vmem],
        out_shape=[
            jax.ShapeDtypeStruct((QUARTER, width), F32),
            jax.ShapeDtypeStruct((QUARTER, depth), BF16),
        ],
        scratch_shapes=[
            pltpu.VMEM((len(weights), depth, width), BF16),
            pltpu.SemaphoreType.DMA((len(weights),)),
        ],
        compiler_params=pltpu.CompilerParams(vmem_limit_bytes=40 * 1024 * 1024),
        cost_estimate=SMALL,
        name="finish",
    )(offsets, pack, back, *weights)


def last_kernel(total_ref, rows_ref, weight_ref, out_ref):
    part = jnp.dot(rows_ref[...], weight_ref[...], preferred_element_type=F32)
    out_ref[...] = (total_ref[...] + part).astype(BF16)


def add_last(total, rows, weight):
    width = 512
    column = lambda i: (0, i)
    return pl.pallas_call(
        last_kernel,
        grid=(total.shape[1] // width,),
        in_specs=[
            pl.BlockSpec((QUARTER, width), column),
            pl.BlockSpec(rows.shape, lambda i: (0, 0)),
            pl.BlockSpec((weight.shape[0], width), column),
        ],
        out_specs=pl.BlockSpec((QUARTER, width), column),
        out_shape=jax.ShapeDtypeStruct(total.shape, BF16),
        compiler_params=pltpu.CompilerParams(vmem_limit_bytes=LESS_VMEM_BYTES),
        cost_estimate=SMALL,
        name="add_last",
    )(total, rows, weight)


def swap(shard, axis, bits):
    return lax.ppermute(shard, axis, [(i, i ^ bits) for i in range(lax.axis_size(axis))])


def local(queries, keys, values, offsets, out_weight):
    n_tp, n_ctx = lax.axis_size("tp"), lax.axis_size("ctx")
    offsets = offsets.T
    segments = [[s * SEGMENT + i for i in range(SEGMENT)] for s in range(n_ctx // SEGMENT)]
    owners = [[c * n_tp + t for t in range(n_tp) for c in segment] for segment in segments]
    across = [(c * n_tp + t, (c ^ (t & 1)) * n_tp + (t ^ 2)) for c in range(n_ctx) for t in range(n_tp)]

    picked = pick(queries, keys, values, offsets)
    picked, sent_weight = lax.optimization_barrier((picked, out_weight))
    sent = lax.all_to_all(picked, "ctx", 0, 0, axis_index_groups=segments, tiled=True)
    weight_2 = lax.ppermute(sent_weight, ("ctx", "tp"), across)
    pack = local_attention(queries, keys, values)
    sent, pack = lax.optimization_barrier((sent, pack))

    first = sent[:, NEAR_ROWS:PICKED, :].reshape(SEGMENT * FAR_ROWS, PAIR)
    second = swap(first, "ctx", 8)
    first = [first] + [swap(first, "ctx", 16 * i) for i in (1, 2, 3)]
    pack = lax.all_to_all(pack, "tp", 0, 0, tiled=True)
    second, near_sent = lax.optimization_barrier((second, sent))
    near_back = near_attention(near_sent)
    second = [second] + [swap(second, "ctx", 16 * i) for i in (1, 2, 3)]
    held = first_far_attention(sent, first)
    held, near_back, sent_weight = lax.optimization_barrier((held, near_back, out_weight))
    weight_1 = swap(sent_weight, "tp", 1)
    held, second = lax.optimization_barrier((held, second))
    back = second_far_attention(sent, near_back, held, second)
    back, pack = lax.optimization_barrier((back, pack))
    back = lax.all_to_all(back, ("ctx", "tp"), 0, 0, axis_index_groups=owners, tiled=True)
    back, weight_2 = lax.optimization_barrier((back, weight_2))
    weight_3 = swap(weight_2, "tp", 1)
    total, rows = finish(offsets, pack, back, [out_weight, weight_1, weight_2])
    return add_last(total, rows, weight_3)


def solution(mesh):
    return jax.shard_map(
        local,
        mesh=mesh,
        in_specs=(P("ctx", "tp"), P("ctx", "tp"), P("ctx", "tp"), P(), P("tp", None)),
        out_specs=P(("ctx", "tp"), None),
        check_vma=False,
    )
```

```python
import functools

import jax
import jax.numpy as jnp
from jax import lax
from jax.experimental import pallas as pl
from jax.experimental.pallas import tpu as pltpu
from jax.sharding import PartitionSpec as P

HEAD_DIM = 64
NEAR_DILATION = 8
FAR_DILATION = 16
SEGMENT = 8
ROWS = 1024
NEAR_ROWS = ROWS // NEAR_DILATION
FAR_ROWS = ROWS // FAR_DILATION
QUARTER = ROWS // 4
NEAR_PART = QUARTER // NEAR_DILATION
FAR_PART = QUARTER // FAR_DILATION
QUARTER_PICKED = NEAR_PART + FAR_PART
PICKED = NEAR_ROWS + FAR_ROWS
SENT_ROWS = PICKED + PICKED // 2
PAIR = 2 * HEAD_DIM
NEG = -1e30
SCALE = HEAD_DIM ** -0.5
BF16 = jnp.bfloat16
F32 = jnp.float32
ROW_BLOCK = 128
VMEM_BYTES = 56 * 1024 * 1024
LESS_VMEM_BYTES = 20 * 1024 * 1024
SMALL = pl.CostEstimate(flops=1000, bytes_accessed=1000, transcendentals=0)


def lanes(shape):
    return lax.broadcasted_iota(jnp.int32, shape, 1)


def head_offsets(offsets_ref, head):
    near = lax.rem(offsets_ref[0, head], NEAR_DILATION)
    return near, lax.rem(offsets_ref[1, head], FAR_DILATION)


def one_hot(offset_near, offset_far):
    row = lax.broadcasted_iota(jnp.int32, (QUARTER_PICKED, QUARTER), 0)
    col = lax.broadcasted_iota(jnp.int32, (QUARTER_PICKED, QUARTER), 1)
    count = QUARTER // NEAR_DILATION
    at = jnp.where(
        row < count,
        row * NEAR_DILATION + offset_near,
        (row - count) * FAR_DILATION + offset_far,
    )
    return jnp.where(col == at, 1.0, 0.0).astype(BF16)


def pick_kernel(offsets_ref, q_ref, k_ref, v_ref, out_ref):
    heads = 2 * pl.num_programs(0)
    first = lax.axis_index("tp") * heads + 2 * pl.program_id(0)
    chosen = jnp.concatenate([one_hot(*head_offsets(offsets_ref, first + i)) for i in range(2)], 0)
    split = QUARTER // NEAR_DILATION
    found = []
    for i in range(ROWS // QUARTER):
        block = slice(i * QUARTER, (i + 1) * QUARTER)
        fields = jnp.concatenate([q_ref[block, :], k_ref[block, :], v_ref[block, :]], 1)
        found.append(jnp.dot(chosen, fields, preferred_element_type=F32))
    low = lanes((PICKED, PAIR)) < HEAD_DIM
    for side in range(2):
        base = side * QUARTER_PICKED
        part = jnp.concatenate(
            [f[base : base + split] for f in found]
            + [f[base + split : base + QUARTER_PICKED] for f in found],
            0,
        )
        q, k, v = (part[:, i * PAIR : (i + 1) * PAIR] for i in range(3))
        if side == 0:
            kv = jnp.where(low, k, pltpu.roll(v, HEAD_DIM, 1))
        else:
            kv = jnp.where(low, pltpu.roll(k, HEAD_DIM, 1), v)
        other = pltpu.roll(q, HEAD_DIM, 1)
        q_low, q_high = (q, other) if side == 0 else (other, q)
        q_packed = []
        for start, count in ((0, NEAR_ROWS), (NEAR_ROWS, FAR_ROWS)):
            half = count // 2
            q_packed.append(
                jnp.where(
                    lanes((half, PAIR)) < HEAD_DIM,
                    q_low[start : start + half],
                    q_high[start + half : start + count],
                )
            )
        out_ref[side, 0:PICKED, :] = kv.astype(BF16)
        out_ref[side, PICKED:SENT_ROWS, :] = (jnp.concatenate(q_packed, 0) * SCALE).astype(BF16)


def pick(queries, keys, values, offsets):
    heads = queries.shape[1] // HEAD_DIM
    pair_spec = pl.BlockSpec((ROWS, PAIR), lambda i: (0, i))
    return pl.pallas_call(
        pick_kernel,
        grid=(heads // 2,),
        in_specs=[pl.BlockSpec(memory_space=pltpu.SMEM)] + [pair_spec] * 3,
        out_specs=pl.BlockSpec((2, SENT_ROWS, PAIR), lambda i: (i, 0, 0)),
        out_shape=jax.ShapeDtypeStruct((heads, SENT_ROWS, PAIR), BF16),
        compiler_params=pltpu.CompilerParams(vmem_limit_bytes=VMEM_BYTES),
        cost_estimate=SMALL,
        name="pick_rows",
    )(offsets, queries, keys, values)


def contract_lanes(a, b):
    return lax.dot_general(a, b, (((1,), (1,)), ((), ())), preferred_element_type=F32)


def with_ones(v):
    return jnp.concatenate([v, jnp.ones_like(v)], 1)


def softmax_sum(scores, values):
    peak = functools.reduce(jnp.maximum, [jnp.max(s, axis=1, keepdims=True) for s in scores])
    acc = None
    for s, v in zip(scores, values):
        part = jnp.dot(jnp.exp(s - peak).astype(BF16), v, preferred_element_type=F32)
        acc = part if acc is None else acc + part
    total = acc[:, PAIR:]
    return acc[:, :PAIR] / total, peak + jnp.log(total)


def local_kernel(q_ref, k_ref, v_ref, pack_ref):
    pair = pl.program_id(0)
    keys = k_ref[...]
    values = with_ones(v_ref[...])
    low = lanes((ROW_BLOCK, PAIR)) < HEAD_DIM
    lane = lanes((ROW_BLOCK, PAIR))
    zero = jnp.zeros((), BF16)
    columns = pl.ds(pl.multiple_of(pair * PAIR, PAIR), PAIR)
    stats_at = pack_ref.shape[1] - PAIR
    for i in range(ROWS // ROW_BLOCK):
        rows = pl.ds(i * ROW_BLOCK, ROW_BLOCK)
        q = q_ref[rows, :] * jnp.asarray(SCALE, BF16)
        both = [
            softmax_sum([contract_lanes(jnp.where(mine, q, zero), keys)], [values])
            for mine in (low, jnp.logical_not(low))
        ]
        pack_ref[rows, columns] = jnp.where(low, both[0][0], both[1][0]).astype(BF16)
        lse = jnp.where((lane & 1) == 0, both[0][1], both[1][1])
        high = lse.astype(BF16)
        rest = (lse - high.astype(F32)).astype(BF16)
        stats = jnp.where(low, high.astype(F32), rest.astype(F32))
        held = pack_ref[rows, stats_at:].astype(F32)
        mine = (lane & (HEAD_DIM - 1)) // 2 == pair
        pack_ref[rows, stats_at:] = jnp.where(
            mine, stats, jnp.where(pair == 0, 0.0, held)
        ).astype(BF16)


def local_attention(queries, keys, values):
    spec = pl.BlockSpec((ROWS, PAIR), lambda i: (0, i))
    width = queries.shape[1] + PAIR
    return pl.pallas_call(
        local_kernel,
        grid=(queries.shape[1] // PAIR,),
        in_specs=[spec] * 3,
        out_specs=pl.BlockSpec((ROWS, width), lambda i: (0, 0)),
        out_shape=jax.ShapeDtypeStruct((ROWS, width), BF16),
        compiler_params=pltpu.CompilerParams(vmem_limit_bytes=VMEM_BYTES),
        cost_estimate=SMALL,
        name="local_attention",
    )(queries, keys, values)


def unpack_queries(packed):
    low = lanes(packed.shape) < HEAD_DIM
    wide = packed.astype(F32)
    top = jnp.where(low, wide, 0.0).astype(BF16)
    bottom = jnp.where(low, pltpu.roll(wide, HEAD_DIM, 1), 0.0).astype(BF16)
    return top, bottom


def result_rows(out, lse):
    high = lse.astype(BF16)
    rest = (lse - high.astype(F32)).astype(BF16)
    lane = lanes(out.shape)
    moved = pltpu.roll(out, HEAD_DIM, 1)
    stats = jnp.where(lane < HEAD_DIM + HEAD_DIM // 2, high.astype(F32), rest.astype(F32))
    return jnp.where(lane < HEAD_DIM, moved, stats).astype(BF16)


def near_kernel(sent_ref, out_ref):
    near_kv = jnp.concatenate([sent_ref[i, 0:NEAR_ROWS, :] for i in range(SEGMENT)], 0)
    near_values = with_ones(near_kv)
    half = NEAR_ROWS // 2
    for i in range(SEGMENT):
        q = jnp.concatenate(unpack_queries(sent_ref[i, PICKED : PICKED + half, :]), 0)
        res = result_rows(*softmax_sum([contract_lanes(q, near_kv)], [near_values]))
        for t in range(4):
            out_ref[t * SEGMENT + i] = res[t * NEAR_PART : (t + 1) * NEAR_PART]


def far_queries(sent_ref, i):
    half = FAR_ROWS // 2
    packed = jnp.concatenate(
        [sent_ref[2 * i + j, SENT_ROWS - half : SENT_ROWS, :] for j in range(2)], 0
    )
    return jnp.concatenate(unpack_queries(packed), 0)


def first_far_kernel(sent_ref, far0_ref, far1_ref, far2_ref, far3_ref, out_ref, lse_ref):
    far = [r[...] for r in (far0_ref, far1_ref, far2_ref, far3_ref)]
    far_values = [with_ones(f) for f in far]
    for i in range(SEGMENT // 2):
        q = far_queries(sent_ref, i)
        out, lse = softmax_sum([contract_lanes(q, f) for f in far], far_values)
        rows = slice(i * PAIR, (i + 1) * PAIR)
        out_ref[rows, :] = out
        lse_ref[rows, :] = lse


def second_far_kernel(
    sent_ref, near_ref, held_ref, held_lse_ref, far0_ref, far1_ref, far2_ref, far3_ref, out_ref
):
    far = [r[...] for r in (far0_ref, far1_ref, far2_ref, far3_ref)]
    far_values = [with_ones(f) for f in far]
    half = FAR_ROWS // 2
    out_ref[:, 0:NEAR_PART, :] = near_ref[...]
    for i in range(SEGMENT // 2):
        q = far_queries(sent_ref, i)
        out, lse = softmax_sum([contract_lanes(q, f) for f in far], far_values)
        rows = slice(i * PAIR, (i + 1) * PAIR)
        held, held_lse = held_ref[rows, :], held_lse_ref[rows, :]
        peak = jnp.maximum(lse, held_lse)
        new, old = jnp.exp(lse - peak), jnp.exp(held_lse - peak)
        both = new + old
        res = result_rows((new * out + old * held) / both, peak + jnp.log(both))
        for t in range(4):
            for j in range(2):
                at = ((t // 2) * 2 + j) * half + (t % 2) * FAR_PART
                out_ref[t * SEGMENT + 2 * i + j, NEAR_PART:, :] = res[at : at + FAR_PART]


def near_attention(sent):
    return pl.pallas_call(
        near_kernel,
        in_specs=[pl.BlockSpec(memory_space=pltpu.VMEM)],
        out_specs=pl.BlockSpec(memory_space=pltpu.VMEM),
        out_shape=jax.ShapeDtypeStruct((4 * SEGMENT, NEAR_PART, PAIR), BF16),
        compiler_params=pltpu.CompilerParams(vmem_limit_bytes=LESS_VMEM_BYTES),
        cost_estimate=SMALL,
        name="near_attention",
    )(sent)


def first_far_attention(sent, far):
    return pl.pallas_call(
        first_far_kernel,
        in_specs=[pl.BlockSpec(memory_space=pltpu.VMEM)] * 5,
        out_specs=[pl.BlockSpec(memory_space=pltpu.VMEM)] * 2,
        out_shape=[jax.ShapeDtypeStruct((SEGMENT * FAR_ROWS, PAIR), F32)] * 2,
        compiler_params=pltpu.CompilerParams(vmem_limit_bytes=LESS_VMEM_BYTES),
        cost_estimate=SMALL,
        name="first_far_attention",
    )(sent, *far)


def second_far_attention(sent, near_back, held, far):
    return pl.pallas_call(
        second_far_kernel,
        in_specs=[pl.BlockSpec(memory_space=pltpu.VMEM)] * 8,
        out_specs=pl.BlockSpec(memory_space=pltpu.VMEM),
        out_shape=jax.ShapeDtypeStruct((4 * SEGMENT, QUARTER_PICKED, PAIR), BF16),
        compiler_params=pltpu.CompilerParams(vmem_limit_bytes=LESS_VMEM_BYTES),
        cost_estimate=SMALL,
        name="second_far_attention",
    )(sent, near_back, *held, *far)


def combine_pair(offsets_ref, back_ref, head, out, lse, low_rows, position):
    outs, lses = [out], [lse]
    offsets = [head_offsets(offsets_ref, head + side) for side in range(2)]
    for which, (start, count, dilation) in enumerate(
        ((0, NEAR_PART, NEAR_DILATION), (NEAR_PART, FAR_PART, FAR_DILATION))
    ):
        offset = [o[which] for o in offsets]
        row = lax.broadcasted_iota(jnp.int32, (QUARTER, 4 * count), 0)
        col = lax.broadcasted_iota(jnp.int32, (QUARTER, 4 * count), 1)
        at = (col & (count - 1)) * dilation + jnp.where((col & count) == 0, offset[0], offset[1])
        placed = jnp.where(row == at, 1.0, 0.0).astype(BF16)
        low = lanes((count, PAIR)) < HEAD_DIM
        first = back_ref[head, start : start + count, :].astype(F32)
        second = back_ref[head + 1, start : start + count, :].astype(F32)
        zero = jnp.zeros((count, PAIR), F32)
        moved = pltpu.roll(second, HEAD_DIM, 1)
        content = [
            (jnp.where(low, first, zero), jnp.where(low, first[:, 64:65], zero)),
            (jnp.where(low, zero, moved), jnp.where(low, zero, second[:, 64:65])),
            (zero, jnp.where(low, first[:, 96:97], zero)),
            (zero, jnp.where(low, zero, second[:, 96:97])),
        ]
        content = jnp.concatenate([jnp.concatenate(part, 1) for part in content], 0)
        wide = jnp.dot(
            placed, content.astype(BF16), preferred_element_type=F32
        )
        here = jnp.where(low_rows, offset[0], offset[1])
        hit = (position & (dilation - 1)) == here
        outs.append(wide[:, :PAIR])
        lses.append(jnp.where(hit, wide[:, PAIR:], NEG))
    peak = jnp.maximum(jnp.maximum(lses[0], lses[1]), lses[2])
    numer, denom = 0.0, 0.0
    for out, lse in zip(outs, lses):
        weight = jnp.exp(lse - peak)
        numer = numer + weight * out
        denom = denom + weight
    return (numer / denom).astype(BF16)


def finish_kernel(offsets_ref, pack_ref, back_ref, *refs):
    weight_refs, (total_ref, last_ref, held, sems) = refs[:-4], refs[-4:]
    depth = held.shape[1]
    copies = [
        pltpu.make_async_copy(weight, held.at[i], sems.at[i]) for i, weight in enumerate(weight_refs)
    ]
    for copy in copies:
        copy.start()
    place = lax.axis_index("tp")
    heads = depth // HEAD_DIM
    low_rows = lanes((QUARTER, PAIR)) < HEAD_DIM
    position = lax.broadcasted_iota(jnp.int32, (QUARTER, PAIR), 0)
    source = lax.broadcasted_iota(jnp.int32, (PAIR, depth), 0) & (HEAD_DIM - 1)
    widen = jnp.where(source == lanes((PAIR, depth)) // HEAD_DIM, 1.0, 0.0).astype(BF16)
    for i in range(4):
        who = place ^ i
        rows = pl.ds(pl.multiple_of(who * QUARTER, QUARTER), QUARTER)
        lse = jnp.dot(pack_ref[rows, depth:], widen, preferred_element_type=F32)
        attn = []
        for pair in range(depth // PAIR):
            columns = slice(pair * PAIR, (pair + 1) * PAIR)
            attn.append(
                combine_pair(
                    offsets_ref,
                    back_ref,
                    who * heads + 2 * pair,
                    pack_ref[rows, columns].astype(F32),
                    lse[:, columns],
                    low_rows,
                    position,
                )
            )
        attn = jnp.concatenate(attn, 1)
        if i == 3:
            last_ref[...] = attn
            continue
        copies[i].wait()
        for start in range(0, total_ref.shape[1], 512):
            columns = slice(start, start + 512)
            part = jnp.dot(attn, held[i, :, columns], preferred_element_type=F32)
            if i > 0:
                part = part + total_ref[:, columns]
            total_ref[:, columns] = part


def finish(offsets, pack, back, weights):
    depth, width = weights[0].shape
    vmem = pl.BlockSpec(memory_space=pltpu.VMEM)
    return pl.pallas_call(
        finish_kernel,
        in_specs=[pl.BlockSpec(memory_space=pltpu.SMEM), vmem, vmem]
        + [pl.BlockSpec(memory_space=pl.ANY)] * len(weights),
        out_specs=[vmem, vmem],
        out_shape=[
            jax.ShapeDtypeStruct((QUARTER, width), F32),
            jax.ShapeDtypeStruct((QUARTER, depth), BF16),
        ],
        scratch_shapes=[
            pltpu.VMEM((len(weights), depth, width), BF16),
            pltpu.SemaphoreType.DMA((len(weights),)),
        ],
        compiler_params=pltpu.CompilerParams(vmem_limit_bytes=40 * 1024 * 1024),
        cost_estimate=SMALL,
        name="finish",
    )(offsets, pack, back, *weights)


def last_kernel(total_ref, rows_ref, weight_ref, out_ref):
    rows = rows_ref[...]
    for start in range(0, out_ref.shape[1], 512):
        columns = slice(start, start + 512)
        part = jnp.dot(rows, weight_ref[:, columns], preferred_element_type=F32)
        out_ref[:, columns] = (total_ref[:, columns] + part).astype(BF16)


def add_last(total, rows, weight):
    vmem = pl.BlockSpec(memory_space=pltpu.VMEM)
    return pl.pallas_call(
        last_kernel,
        in_specs=[vmem] * 3,
        out_specs=vmem,
        out_shape=jax.ShapeDtypeStruct(total.shape, BF16),
        compiler_params=pltpu.CompilerParams(vmem_limit_bytes=LESS_VMEM_BYTES),
        cost_estimate=SMALL,
        name="add_last",
    )(total, rows, weight)


def swap(shard, axis, bits):
    return lax.ppermute(shard, axis, [(i, i ^ bits) for i in range(lax.axis_size(axis))])


def local(queries, keys, values, offsets, out_weight):
    n_tp, n_ctx = lax.axis_size("tp"), lax.axis_size("ctx")
    offsets = offsets.T
    segments = [[s * SEGMENT + i for i in range(SEGMENT)] for s in range(n_ctx // SEGMENT)]
    owners = [[c * n_tp + t for t in range(n_tp) for c in segment] for segment in segments]
    across = [(c * n_tp + t, (c ^ (t & 1)) * n_tp + (t ^ 2)) for c in range(n_ctx) for t in range(n_tp)]

    picked = pick(queries, keys, values, offsets)
    picked, sent_weight = lax.optimization_barrier((picked, out_weight))
    sent = lax.all_to_all(picked, "ctx", 0, 0, axis_index_groups=segments, tiled=True)
    weight_2 = lax.ppermute(sent_weight, ("ctx", "tp"), across)
    pack = local_attention(queries, keys, values)
    sent, pack = lax.optimization_barrier((sent, pack))

    first = sent[:, NEAR_ROWS:PICKED, :].reshape(SEGMENT * FAR_ROWS, PAIR)
    second = swap(first, "ctx", 8)
    first = [first] + [swap(first, "ctx", 16 * i) for i in (1, 2, 3)]
    pack = lax.all_to_all(pack, "tp", 0, 0, tiled=True)
    second, near_sent = lax.optimization_barrier((second, sent))
    near_back = near_attention(near_sent)
    second = [second] + [swap(second, "ctx", 16 * i) for i in (1, 2, 3)]
    held = first_far_attention(sent, first)
    held, near_back, sent_weight = lax.optimization_barrier((held, near_back, out_weight))
    weight_1 = swap(sent_weight, "tp", 1)
    held, second = lax.optimization_barrier((held, second))
    back = second_far_attention(sent, near_back, held, second)
    back, pack = lax.optimization_barrier((back, pack))
    back = lax.all_to_all(back, ("ctx", "tp"), 0, 0, axis_index_groups=owners, tiled=True)
    back, weight_2 = lax.optimization_barrier((back, weight_2))
    weight_3 = swap(weight_2, "tp", 1)
    total, rows = finish(offsets, pack, back, [out_weight, weight_1, weight_2])
    return add_last(total, rows, weight_3)


def solution(mesh):
    return jax.shard_map(
        local,
        mesh=mesh,
        in_specs=(P("ctx", "tp"), P("ctx", "tp"), P("ctx", "tp"), P(), P("tp", None)),
        out_specs=P(("ctx", "tp"), None),
        check_vma=False,
    )
```
